32 devices in a mesh: grp: 4 (over y, x), tok: 8 (over z, core).
Axes of the slice: x: 2, y: 2, z: 4, core: 2. Of those that a mesh axis runs over, the one named last changes fastest.
Arguments:
- tokens: bfloat16 [4096, 2560], P(('grp', 'tok')), may hold values from -6 to 6
- input_gain: bfloat16 [2560], replicated, may hold values from 0.25 to 1.75
- query_down: bfloat16 [2560, 768], replicated, may hold values from -0.125 to 0.125
- query_gain: bfloat16 [768], replicated, may hold values from 0.25 to 1.75
- query_up: bfloat16 [768, 1920], replicated, may hold values from -0.21875 to 0.21875
- latent_down: bfloat16 [2560, 288], replicated, may hold values from -0.125 to 0.125
- latent_gain: bfloat16 [256], replicated, may hold values from 0.25 to 1.75
- key_up: bfloat16 [256, 1280], replicated, may hold values from -0.375 to 0.375
- value_up: bfloat16 [256, 1280], replicated, may hold values from -0.375 to 0.375
- output_weight: bfloat16 [1280, 2560], replicated, may hold values from -0.15625 to 0.15625
- post_gain: bfloat16 [2560], replicated, may hold values from 0.25 to 1.75
- gate_weight: bfloat16 [2560, 3200], P('tok', 'grp'), may hold values from -0.125 to 0.125
- up_weight: bfloat16 [2560, 3200], P('tok', 'grp'), may hold values from -0.125 to 0.125
- down_weight: bfloat16 [3200, 2560], P('grp', 'tok'), may hold values from -0.109375 to 0.109375
- cache_latents: bfloat16 [4, 4096, 288], P('grp', 'tok'), as said below
- prompt_latents: bfloat16 [8, 1024, 288], P(None, 'tok'), as said below
- cache_len: int32 [4], replicated, may hold values from 1 to 4096, 8192 in all
- prompt_len: int32 [8], replicated, may hold values from 1 to 1024, 4096 in all
- prompt_of: int32 [4], replicated, may hold values from 0 to 7
Outputs:
- layer_out: bfloat16 [4096, 2560], P(('grp', 'tok'))
- new_latents: bfloat16 [4096, 288], P(('grp', 'tok'))
The draws below stay inside these ranges and needn't reach their ends.
Inputs may be any that keep to these rules, and one draw needn't show every extreme that they name: `cache_len`: some request has exactly 4096 live cached rows. `prompt_len`: some stored prompt has exactly 1024 live rows. `cache_latents`: rows past a request's live length are stored but never read. `prompt_latents`: rows past a prompt's live length are stored but never read.
All inputs are finite; a program needn't handle non-finite values.
Results may differ from the reference program's by a relative error of at most 0.02.
Values may be sent and summed in bfloat16 or wider, within the bound.
A program may use at most 128 MiB of HBM per device.

```python
import math
import jax
import jax.numpy as jnp
import numpy as np
from jax import lax

D = 2560
QR = 768
KVR = 256
HEADS = 20
NOPE = 64
ROPE = 32
VDIM = 64
FF = 3200
SPAN = 1024
CACHE = 4096
PLEN = 1024
NPROMPT = 8
TOK_DEV = 128
REQ_GRP = 1
REQS = 4
TOKENS = 4096
N_TOK = 8


def latent_rows(key, shape):
    values = jax.random.normal(key, shape, jnp.float32)
    return values.astype(jnp.bfloat16)


def draw_cache_latents(key, part):
    return latent_rows(jax.random.fold_in(key, 11), (REQS, CACHE, KVR + ROPE))


def draw_prompt_latents(key, part):
    return latent_rows(jax.random.fold_in(key, 23), (NPROMPT, PLEN, KVR + ROPE))


def place_ends(result, stream_key, low, largest):
    spot = [jax.random.randint(jax.random.fold_in(stream_key, axis), (), 0, length) for axis, length in enumerate(result.shape)]
    longest = result.shape.index(max(result.shape))
    beside = spot[:longest] + [(spot[longest] + 1) % result.shape[longest]] + spot[longest + 1:]
    return result.at[tuple(spot)].set(low).at[tuple(beside)].set(largest)


def steps_of(key, shape, cuts, smallest, top_value):
    def one(axis_at, shards_of):
        draws = jax.random.uniform(jax.random.fold_in(jax.random.fold_in(key, 6), axis_at), (shards_of,), jnp.float32, smallest / len(cuts), top_value / len(cuts))
        return jnp.repeat(jnp.exp(draws), shape[axis_at] // shards_of).reshape((-1,) + (1,) * (len(shape) - axis_at - 1))

    level = one(*cuts[0])
    for cut in cuts[1:]:
        level = level * one(*cut)
    return level


def length_profile(amount, total, reach, slope):
    portions = [(1 << 20) // math.isqrt(grade ** slope) + 1 for grade in range(2, amount + 1)]
    spare, counts = total - reach - (amount - 1), [1] * (amount - 1)
    while spare > 0:
        free = [i for i in range(amount - 1) if counts[i] < reach]
        pool, left = sum([portions[i] for i in free]), spare
        for i in free:
            addition = min(reach - counts[i], max(1, left * portions[i] // pool), spare)
            counts[i] = counts[i] + addition
            spare = spare - addition
    return np.array([reach] + counts)


def uneven_parts(key, count, total, most, slope):
    if count == 2:
        one = jax.random.randint(key, (), max(1, total - most), min(most, total - 1) + 1)
        return jnp.stack([one, total - one])
    sizes = jnp.asarray(length_profile(count, total, most, slope), jnp.int32)
    couples = (count - 1) // 2
    source_of, sink = sizes[1:1 + 2 * couples:2], sizes[2:2 + 2 * couples:2]
    slack = jnp.minimum(source_of - 1, most - sink)
    passed = jax.random.randint(jax.random.fold_in(key, 1), (couples,), 0, 1 << 20) % (slack + 1)
    sizes = sizes.at[1:1 + 2 * couples:2].set(source_of - passed).at[2:2 + 2 * couples:2].set(sink + passed)
    return sizes[jax.random.permutation(jax.random.fold_in(key, 2), count)]


def centred(rng, extent, scale, most, pieces=(), kind=jnp.bfloat16):
    array = jax.random.normal(rng, extent, jnp.float32) * scale
    if len(pieces) > 0:
        array = steps_of(rng, extent, pieces, -0.22, 0.18) * array
    return jnp.clip(array, min=-most, max=most).astype(kind)


def setup_inputs(seed: int = 0) -> dict:
    arg_keys = jax.random.split(jax.random.key(seed), 20)
    return {
        "tokens": centred(arg_keys[0], (TOKENS, D), 1.0, 6.0, ((0, 32),)),
        "input_gain": jnp.clip(1.0 + 0.15 * jax.random.normal(arg_keys[1], (D,), jnp.float32), 0.25, 1.75).astype(jnp.bfloat16),
        "query_down": centred(arg_keys[2], (D, QR), D ** -0.5, 0.125),
        "query_gain": jnp.clip(1.0 + 0.15 * jax.random.normal(arg_keys[3], (QR,), jnp.float32), 0.25, 1.75).astype(jnp.bfloat16),
        "query_up": centred(arg_keys[4], (QR, HEADS * (NOPE + ROPE)), QR ** -0.5, 0.21875),
        "latent_down": centred(arg_keys[5], (D, KVR + ROPE), D ** -0.5, 0.125),
        "latent_gain": jnp.clip(1.0 + 0.15 * jax.random.normal(arg_keys[6], (KVR,), jnp.float32), 0.25, 1.75).astype(jnp.bfloat16),
        "key_up": centred(arg_keys[7], (KVR, HEADS * NOPE), KVR ** -0.5, 0.375),
        "value_up": centred(arg_keys[8], (KVR, HEADS * VDIM), KVR ** -0.5, 0.375),
        "output_weight": centred(arg_keys[9], (HEADS * VDIM, D), (HEADS * VDIM) ** -0.5, 0.15625),
        "post_gain": jnp.clip(1.0 + 0.15 * jax.random.normal(arg_keys[10], (D,), jnp.float32), 0.25, 1.75).astype(jnp.bfloat16),
        "gate_weight": centred(arg_keys[11], (D, FF), D ** -0.5, 0.125, ((0, 8), (1, 4))),
        "up_weight": centred(arg_keys[12], (D, FF), D ** -0.5, 0.125, ((0, 8), (1, 4))),
        "down_weight": centred(arg_keys[13], (FF, D), FF ** -0.5, 0.109375, ((0, 4), (1, 8))),
        "cache_latents": draw_cache_latents(jax.random.fold_in(arg_keys[19], 71), 0),
        "prompt_latents": draw_prompt_latents(jax.random.fold_in(arg_keys[19], 71), 0),
        "cache_len": uneven_parts(arg_keys[16], REQS, REQS * CACHE // 2, CACHE, 1).astype(jnp.int32),
        "prompt_len": uneven_parts(arg_keys[17], NPROMPT, NPROMPT * PLEN // 2, PLEN, 1).astype(jnp.int32),
        "prompt_of": place_ends(jax.random.randint(arg_keys[18], (REQS,), 0, NPROMPT), jax.random.fold_in(arg_keys[18], 1), 0, NPROMPT - 1).astype(jnp.int32),
    }


EPSILON = 1e-06

def rounded(values):
    return lax.optimization_barrier(values.astype(jnp.bfloat16))

def norm_rows(values, gain_vector):
    mean_square = lax.optimization_barrier(jnp.mean(values * values, axis=-1, keepdims=True))
    return values * lax.rsqrt(mean_square + EPSILON) * gain_vector.astype(jnp.float32)

def rotate(values, positions):
    half_width = values.shape[-1] // 2
    frequency = 10000.0 ** (-jnp.arange(half_width, dtype=jnp.float32) / half_width)
    angles = positions.astype(jnp.float32)[:, None] * frequency[None, :]
    if values.ndim == 3:
        angles = angles[:, None, :]
    cosine = jnp.cos(angles)
    sine_part = jnp.sin(angles)
    leading = values[..., :half_width]
    trailing = values[..., half_width:]
    return jnp.concatenate([leading * cosine - trailing * sine_part, trailing * cosine + leading * sine_part], axis=-1)

def reference(tokens, input_gain, query_down, query_gain, query_up, latent_down, latent_gain, key_up, value_up, output_weight, post_gain, gate_weight, up_weight, down_weight, cache_latents, prompt_latents, cache_len, prompt_len, prompt_of):
    token_count = tokens.shape[0]
    token_index = jnp.arange(token_count, dtype=jnp.int32)
    block_index_all = (token_index // TOK_DEV).astype(jnp.int32)
    row_in_block = (token_index % TOK_DEV).astype(jnp.int32)
    group_of = (block_index_all // N_TOK).astype(jnp.int32)
    shard_of = (block_index_all % N_TOK).astype(jnp.int32)
    request = (group_of * REQ_GRP + shard_of % REQ_GRP).astype(jnp.int32)
    within = (shard_of // REQ_GRP * TOK_DEV + row_in_block).astype(jnp.int32)
    sorted_index = (request * SPAN + within).astype(jnp.int32)
    slot = jnp.arange(token_count, dtype=jnp.int32)
    slot_request = (slot // SPAN).astype(jnp.int32)
    slot_place = (slot % SPAN).astype(jnp.int32)
    slot_shard = (slot_place // TOK_DEV * REQ_GRP + slot_request % REQ_GRP).astype(jnp.int32)
    order = ((slot_request // REQ_GRP * N_TOK + slot_shard) * TOK_DEV + slot_place % TOK_DEV).astype(jnp.int32)
    own_prompt = prompt_len[prompt_of].astype(jnp.int32)
    positions = (own_prompt[request] + cache_len[request] + within).astype(jnp.int32)
    normed = rounded(norm_rows(tokens.astype(jnp.float32), input_gain))
    query_latent = rounded(norm_rows(jnp.dot(normed, query_down, preferred_element_type=jnp.float32), query_gain))
    query_full = rounded(jnp.dot(query_latent, query_up, preferred_element_type=jnp.float32)).reshape(token_count, HEADS, NOPE + ROPE)
    absorbed = jnp.einsum('thd,khd->thk', query_full[..., :NOPE].astype(jnp.float32), key_up.reshape(KVR, HEADS, NOPE).astype(jnp.float32))
    turned = rotate(query_full[..., NOPE:].astype(jnp.float32), positions)
    queries = rounded(jnp.concatenate([absorbed, turned], axis=-1))
    latent_raw = jnp.dot(normed, latent_down, preferred_element_type=jnp.float32)
    new_latents = rounded(jnp.concatenate([norm_rows(latent_raw[:, :KVR], latent_gain), rotate(latent_raw[:, KVR:], positions)], axis=-1))
    queries_sorted = queries[order]
    latents_sorted = new_latents[order]
    query_block = min(256, SPAN)
    per_request = SPAN // query_block
    request_count = token_count // SPAN
    score_scale = 1.0 / (NOPE + ROPE) ** 0.5
    key_index = jnp.arange(PLEN + CACHE + SPAN, dtype=jnp.int32)

    def attend(block_index):
        owner = (block_index // per_request).astype(jnp.int32)
        first_row = (block_index % per_request * query_block).astype(jnp.int32)
        query_rows = lax.dynamic_slice_in_dim(queries_sorted, (owner * SPAN + first_row).astype(jnp.int32), query_block, 0)
        prompt_rows = lax.dynamic_index_in_dim(prompt_latents, prompt_of[owner], 0, keepdims=False)
        cache_rows = lax.dynamic_index_in_dim(cache_latents, owner, 0, keepdims=False)
        span_rows = lax.dynamic_slice_in_dim(latents_sorted, (owner * SPAN).astype(jnp.int32), SPAN, 0)
        key_rows = jnp.concatenate([prompt_rows, cache_rows, span_rows], axis=0)
        row_place = first_row + jnp.arange(query_block, dtype=jnp.int32)
        live_keys = jnp.where(key_index < PLEN, key_index < own_prompt[owner], jnp.where(key_index < PLEN + CACHE, key_index - PLEN < cache_len[owner], (key_index - PLEN - CACHE)[None, :] <= row_place[:, None]))
        live_keys = jnp.broadcast_to(live_keys, (query_block, PLEN + CACHE + SPAN))
        scores = jnp.einsum('qhw,kw->qhk', query_rows.astype(jnp.float32), key_rows.astype(jnp.float32)) * score_scale
        live_heads = live_keys[:, None, :]
        row_max = lax.optimization_barrier(jnp.max(jnp.where(live_heads, scores, -1e+30), axis=-1, keepdims=True))
        weights = jnp.where(live_heads, jnp.exp(scores - row_max), 0.0)
        row_total = lax.optimization_barrier(jnp.sum(weights, axis=-1, keepdims=True))
        mixed = jnp.einsum('qhk,kc->qhc', rounded(weights).astype(jnp.float32), key_rows[:, :KVR].astype(jnp.float32))
        return rounded(mixed / row_total)
    blocks_all = jnp.arange(request_count * per_request, dtype=jnp.int32)
    latent_sorted = lax.map(attend, blocks_all).reshape(token_count, HEADS, KVR)
    latent_out = latent_sorted[sorted_index]
    heads_out = rounded(jnp.einsum('thk,khv->thv', latent_out.astype(jnp.float32), value_up.reshape(KVR, HEADS, VDIM).astype(jnp.float32))).reshape(token_count, HEADS * VDIM)
    attended = jnp.dot(heads_out, output_weight, preferred_element_type=jnp.float32)
    residual = rounded(tokens.astype(jnp.float32) + attended)
    post_norm = rounded(norm_rows(residual.astype(jnp.float32), post_gain))
    gate_values = jnp.dot(post_norm, gate_weight, preferred_element_type=jnp.float32)
    up_values = jnp.dot(post_norm, up_weight, preferred_element_type=jnp.float32)
    hidden = rounded(jax.nn.silu(gate_values) * up_values)
    down_values = jnp.dot(hidden, down_weight, preferred_element_type=jnp.float32)
    layer_out = (residual.astype(jnp.float32) + down_values).astype(jnp.bfloat16)
    return (layer_out, new_latents)
```

```python
import functools

import jax
import jax.numpy as jnp
from jax import lax
from jax.experimental import pallas as pl
from jax.experimental.pallas import tpu as pltpu
from jax.sharding import PartitionSpec as P

KVR = 256
HEADS = 20
NOPE = 64
ROPE = 32
VDIM = 64
SPAN = 1024
MARK = 384


EPSILON = 1e-06


def norm_rows(values, gain_vector):
    mean_square = jnp.mean(values * values, axis=-1, keepdims=True)
    return values * lax.rsqrt(mean_square + EPSILON) * gain_vector.astype(jnp.float32)


def rotate(values, positions):
    half_width = values.shape[-1] // 2
    frequency = 10000.0 ** (-jnp.arange(half_width, dtype=jnp.float32) / half_width)
    angles = positions.astype(jnp.float32)[:, None] * frequency[None, :]
    if values.ndim == 3:
        angles = angles[:, None, :]
    cosine = jnp.cos(angles)
    sine_part = jnp.sin(angles)
    leading = values[..., :half_width]
    trailing = values[..., half_width:]
    return jnp.concatenate(
        [leading * cosine - trailing * sine_part, trailing * cosine + leading * sine_part], axis=-1
    )


def flash_kernel(row_block, key_block, q_ref, prompt_ref, cache_ref, span_ref, out_ref):
    segments = []
    for ref in (prompt_ref, cache_ref, span_ref):
        for first in range(0, ref.shape[0], key_block):
            segments.append(ref.at[pl.ds(first, min(key_block, ref.shape[0]))])

    @pl.loop(0, q_ref.shape[0] // row_block)
    def _(step):
        rows = pl.ds(pl.multiple_of(step * row_block, row_block), row_block)
        q = q_ref[rows, :]

        def score(keys):
            return lax.dot_general(
                q, keys[...], (((1,), (1,)), ((), ())), preferred_element_type=jnp.float32
            )

        scores = score(segments[0])
        largest = None
        for at, keys in enumerate(segments):
            following = score(segments[at + 1]) if at + 1 < len(segments) else None
            block_max = jnp.max(scores, axis=1, keepdims=True)
            new_max = block_max if at == 0 else jnp.maximum(largest, block_max)
            weights = jnp.exp2(scores - new_max)
            block_sum = jnp.sum(weights, axis=1, keepdims=True)
            product = jnp.dot(
                weights.astype(jnp.bfloat16), keys[:, :KVR], preferred_element_type=jnp.float32
            )
            if at == 0:
                total, mixed = block_sum, product
            else:
                factor = jnp.exp2(largest - new_max)
                total = total * factor + block_sum
                mixed = mixed * factor + product
            largest, scores = new_max, following
        out_ref[rows, :] = (mixed / total).astype(jnp.bfloat16)


def flash(queries, prompt_keys, cache_keys, span_keys):
    rows = queries.shape[0]
    count = prompt_keys.shape[0] + cache_keys.shape[0] + span_keys.shape[0]
    return pl.pallas_call(
        functools.partial(flash_kernel, 512, 512),
        out_shape=jax.ShapeDtypeStruct((rows, KVR), jnp.bfloat16),
        in_specs=[pl.BlockSpec(memory_space=pltpu.VMEM)] * 4,
        out_specs=pl.BlockSpec(memory_space=pltpu.VMEM),
        cost_estimate=pl.CostEstimate(
            flops=2 * rows * count * 768, bytes_accessed=2**24, transcendentals=rows * count
        ),
        compiler_params=pltpu.CompilerParams(vmem_limit_bytes=48 * 2**20),
    )(queries, prompt_keys, cache_keys, span_keys)


def widened(key_rows, live, hidden_at):
    rows = jnp.where(live[:, None], key_rows, jnp.zeros_like(key_rows))
    bias = jnp.where(live, 0.0, -1e30).astype(jnp.bfloat16)[:, None]
    between = jnp.zeros((rows.shape[0], MARK - rows.shape[1] - 1), jnp.bfloat16)
    return jnp.concatenate([rows, bias, between, hidden_at], axis=1)


def body(
    tokens,
    input_gain,
    query_down,
    query_gain,
    query_up,
    latent_down,
    latent_gain,
    key_up,
    value_up,
    output_weight,
    post_gain,
    gate_weight,
    up_weight,
    down_weight,
    cache_latents,
    prompt_latents,
    cache_len,
    prompt_len,
    prompt_of,
):
    group_index = lax.axis_index("grp")
    shard_index = lax.axis_index("tok")
    tok_dev = tokens.shape[0]
    tok_count = lax.axis_size("tok")
    group_requests = tok_dev * tok_count // SPAN
    local_request = shard_index % group_requests
    owner = group_index * group_requests + local_request
    offset = shard_index // group_requests * tok_dev
    within = offset + jnp.arange(tok_dev, dtype=jnp.int32)
    own_prompt = prompt_of[owner]
    prompt_live = prompt_len[own_prompt]
    cache_live = cache_len[owner]
    positions = prompt_live + cache_live + within
    normed = norm_rows(tokens.astype(jnp.float32), input_gain).astype(jnp.bfloat16)
    query_latent = norm_rows(
        jnp.dot(normed, query_down, preferred_element_type=jnp.float32), query_gain
    ).astype(jnp.bfloat16)
    query_full = jnp.dot(query_latent, query_up, preferred_element_type=jnp.float32).astype(
        jnp.bfloat16
    )
    query_full = lax.optimization_barrier(query_full).reshape(tok_dev, HEADS, NOPE + ROPE)
    score_scale = 1.4426950408889634 / (NOPE + ROPE) ** 0.5
    absorbed = jnp.einsum(
        "thd,khd->htk",
        query_full[..., :NOPE],
        key_up.reshape(KVR, HEADS, NOPE),
        preferred_element_type=jnp.float32,
    )
    turned = rotate(query_full[..., NOPE:].astype(jnp.float32), positions).transpose(1, 0, 2)
    queries = (jnp.concatenate([absorbed, turned], axis=-1) * score_scale).astype(jnp.bfloat16)
    marks = jnp.concatenate(
        [
            jnp.ones((tok_dev, 1), jnp.bfloat16),
            jnp.zeros((tok_dev, MARK - KVR - ROPE - 1), jnp.bfloat16),
            jnp.eye(tok_dev, dtype=jnp.bfloat16),
        ],
        axis=1,
    )
    query_rows = jnp.concatenate(
        [queries, jnp.broadcast_to(marks, (HEADS,) + marks.shape)], axis=-1
    ).reshape(HEADS * tok_dev, MARK + tok_dev)
    latent_raw = jnp.dot(normed, latent_down, preferred_element_type=jnp.float32)
    new_latents = jnp.concatenate(
        [norm_rows(latent_raw[:, :KVR], latent_gain), rotate(latent_raw[:, KVR:], positions)],
        axis=-1,
    ).astype(jnp.bfloat16)
    group_prompts = jnp.concatenate(
        [
            lax.dynamic_slice_in_dim(
                prompt_latents, prompt_of[group_index * group_requests + each], 1, 0
            )
            for each in range(group_requests)
        ],
        axis=0,
    )
    cache_all = lax.all_gather(cache_latents, "tok", axis=1, tiled=True)
    prompt_all = lax.all_gather(group_prompts, "tok", axis=1, tiled=True)
    span_all = lax.all_gather(new_latents, "tok", axis=0)
    cache_rows = lax.dynamic_index_in_dim(cache_all, local_request, 0, keepdims=False)
    prompt_rows = lax.dynamic_index_in_dim(prompt_all, local_request, 0, keepdims=False)
    span_rows = lax.dynamic_index_in_dim(
        span_all.reshape(SPAN // tok_dev, group_requests, tok_dev, KVR + ROPE),
        local_request,
        1,
        keepdims=False,
    ).reshape(SPAN, KVR + ROPE)
    span_place = jnp.arange(SPAN, dtype=jnp.int32)
    hidden = jnp.where(span_place[:, None] <= within[None, :], 0.0, -1e30).astype(jnp.bfloat16)
    prompt_live_rows = jnp.arange(prompt_rows.shape[0], dtype=jnp.int32) < prompt_live
    cache_live_rows = jnp.arange(cache_rows.shape[0], dtype=jnp.int32) < cache_live
    latent_out = flash(
        query_rows,
        widened(
            prompt_rows,
            prompt_live_rows,
            jnp.zeros((prompt_rows.shape[0], tok_dev), jnp.bfloat16),
        ),
        widened(
            cache_rows, cache_live_rows, jnp.zeros((cache_rows.shape[0], tok_dev), jnp.bfloat16)
        ),
        widened(span_rows, span_place >= 0, hidden),
    ).reshape(HEADS, tok_dev, KVR)
    heads_out = (
        jnp.einsum(
            "htk,khv->thv",
            latent_out,
            value_up.reshape(KVR, HEADS, VDIM),
            preferred_element_type=jnp.float32,
        )
        .astype(jnp.bfloat16)
        .reshape(tok_dev, HEADS * VDIM)
    )
    attended = jnp.dot(heads_out, output_weight, preferred_element_type=jnp.float32)
    residual = lax.optimization_barrier(
        (tokens.astype(jnp.float32) + attended).astype(jnp.bfloat16)
    )
    post_norm = norm_rows(residual.astype(jnp.float32), post_gain).astype(jnp.bfloat16)
    rows_all = lax.all_gather(post_norm, "grp", axis=0, tiled=True)
    gate_values = jnp.dot(
        rows_all,
        lax.all_gather(gate_weight, "tok", axis=0, tiled=True),
        preferred_element_type=jnp.float32,
    )
    up_values = jnp.dot(
        rows_all,
        lax.all_gather(up_weight, "tok", axis=0, tiled=True),
        preferred_element_type=jnp.float32,
    )
    hidden = (jax.nn.silu(gate_values) * up_values).astype(jnp.bfloat16)
    partial_out = jnp.dot(
        hidden,
        lax.all_gather(down_weight, "tok", axis=1, tiled=True),
        preferred_element_type=jnp.float32,
    )
    down_values = lax.psum_scatter(
        partial_out.astype(jnp.bfloat16), "grp", scatter_dimension=0, tiled=True
    ).astype(jnp.float32)
    layer_out = (residual.astype(jnp.float32) + down_values).astype(jnp.bfloat16)
    return (layer_out, new_latents)


def solution(mesh):
    in_specs = (
        P(("grp", "tok"), None),
        P(),
        P(),
        P(),
        P(),
        P(),
        P(),
        P(),
        P(),
        P(),
        P(),
        P("tok", "grp"),
        P("tok", "grp"),
        P("grp", "tok"),
        P("grp", "tok", None),
        P(None, "tok", None),
        P(),
        P(),
        P(),
    )
    out_specs = (P(("grp", "tok"), None), P(("grp", "tok"), None))
    return jax.shard_map(body, mesh=mesh, in_specs=in_specs, out_specs=out_specs, check_vma=False)
```

```python
import functools

import jax
import jax.numpy as jnp
from jax import lax
from jax.experimental import pallas as pl
from jax.experimental.pallas import tpu as pltpu
from jax.sharding import PartitionSpec as P

KVR = 256
HEADS = 20
NOPE = 64
ROPE = 32
VDIM = 64
SPAN = 1024
MARK = 384


EPSILON = 1e-06


def norm_rows(values, gain_vector):
    mean_square = jnp.mean(values * values, axis=-1, keepdims=True)
    return values * lax.rsqrt(mean_square + EPSILON) * gain_vector.astype(jnp.float32)


def rotate(values, positions):
    half_width = values.shape[-1] // 2
    frequency = 10000.0 ** (-jnp.arange(half_width, dtype=jnp.float32) / half_width)
    angles = positions.astype(jnp.float32)[:, None] * frequency[None, :]
    if values.ndim == 3:
        angles = angles[:, None, :]
    cosine = jnp.cos(angles)
    sine_part = jnp.sin(angles)
    leading = values[..., :half_width]
    trailing = values[..., half_width:]
    return jnp.concatenate(
        [leading * cosine - trailing * sine_part, trailing * cosine + leading * sine_part], axis=-1
    )


def flash_kernel(row_block, key_block, q_ref, prompt_ref, cache_ref, span_ref, out_ref):
    segments = []
    for ref in (prompt_ref, cache_ref, span_ref):
        for first in range(0, ref.shape[0], key_block):
            segments.append(ref.at[pl.ds(first, min(key_block, ref.shape[0]))])

    @pl.loop(0, q_ref.shape[0] // row_block)
    def _(step):
        rows = pl.ds(pl.multiple_of(step * row_block, row_block), row_block)
        q = q_ref[rows, :]

        def score(keys):
            return lax.dot_general(
                q, keys[...], (((1,), (1,)), ((), ())), preferred_element_type=jnp.float32
            )

        scores = score(segments[0])
        largest = None
        for at, keys in enumerate(segments):
            following = score(segments[at + 1]) if at + 1 < len(segments) else None
            block_max = jnp.max(scores, axis=1, keepdims=True)
            new_max = block_max if at == 0 else jnp.maximum(largest, block_max)
            weights = jnp.exp2(scores - new_max)
            block_sum = jnp.sum(weights, axis=1, keepdims=True)
            product = jnp.dot(
                weights.astype(jnp.bfloat16), keys[:, :KVR], preferred_element_type=jnp.float32
            )
            if at == 0:
                total, mixed = block_sum, product
            else:
                factor = jnp.exp2(largest - new_max)
                total = total * factor + block_sum
                mixed = mixed * factor + product
            largest, scores = new_max, following
        out_ref[rows, :] = (mixed / total).astype(jnp.bfloat16)


def flash(queries, prompt_keys, cache_keys, span_keys):
    rows = queries.shape[0]
    count = prompt_keys.shape[0] + cache_keys.shape[0] + span_keys.shape[0]
    return pl.pallas_call(
        functools.partial(flash_kernel, 512, 512),
        out_shape=jax.ShapeDtypeStruct((rows, KVR), jnp.bfloat16),
        in_specs=[pl.BlockSpec(memory_space=pltpu.VMEM)] * 4,
        out_specs=pl.BlockSpec(memory_space=pltpu.VMEM),
        cost_estimate=pl.CostEstimate(
            flops=2 * rows * count * 768, bytes_accessed=2**24, transcendentals=rows * count
        ),
        compiler_params=pltpu.CompilerParams(vmem_limit_bytes=48 * 2**20),
    )(queries, prompt_keys, cache_keys, span_keys)


def feed_forward_kernel(
    post_ref, residual_ref, gate_ref, up_ref, down_ref, out_ref,
    rows_in, part_out, part_in, own, row_send, row_recv, part_send, part_recv,
):
    groups = rows_in.shape[0] + 1
    me = lax.axis_index("grp")

    def device(step):
        return {"grp": lax.rem(me + step + groups, groups)}

    def row_copy(step):
        return pltpu.make_async_remote_copy(
            src_ref=post_ref,
            dst_ref=rows_in.at[step - 1],
            send_sem=row_send.at[step - 1],
            recv_sem=row_recv.at[step - 1],
            device_id=device(step),
            device_id_type=pl.DeviceIdType.MESH,
        )

    def part_copy(step):
        return pltpu.make_async_remote_copy(
            src_ref=part_out.at[step - 1],
            dst_ref=part_in.at[step - 1],
            send_sem=part_send.at[step - 1],
            recv_sem=part_recv.at[step - 1],
            device_id=device(-step),
            device_id_type=pl.DeviceIdType.MESH,
        )

    def layer(rows):
        gate = jnp.dot(rows, gate_ref[...], preferred_element_type=jnp.float32)
        up = jnp.dot(rows, up_ref[...], preferred_element_type=jnp.float32)
        hidden = (gate / (1.0 + jnp.exp(-gate)) * up).astype(jnp.bfloat16)
        return jnp.dot(hidden, down_ref[...], preferred_element_type=jnp.float32)

    barrier = pltpu.get_barrier_semaphore()
    for step in range(1, groups):
        pl.semaphore_signal(
            barrier, inc=1, device_id=device(step), device_id_type=pl.DeviceIdType.MESH
        )
    pl.semaphore_wait(barrier, groups - 1)
    for step in range(1, groups):
        row_copy(step).start()
    own[...] = layer(post_ref[...]) + residual_ref[...].astype(jnp.float32)

    @pl.loop(1, groups)
    def _(step):
        row_copy(step).wait_recv()
        part_out[step - 1] = layer(rows_in[step - 1]).astype(jnp.bfloat16)
        part_copy(step).start()

    @pl.loop(1, groups)
    def _(step):
        part_copy(step).wait_recv()
        own[...] += part_in[step - 1].astype(jnp.float32)
        part_copy(step).wait_send()
        row_copy(step).wait_send()

    out_ref[...] = own[...].astype(jnp.bfloat16)


def feed_forward(post_norm, residual, gate, up, down):
    groups = lax.axis_size("grp")
    slots = (groups - 1,) + post_norm.shape
    return pl.pallas_call(
        feed_forward_kernel,
        out_shape=jax.ShapeDtypeStruct(post_norm.shape, jnp.bfloat16),
        in_specs=[pl.BlockSpec(memory_space=pltpu.VMEM)] * 5,
        out_specs=pl.BlockSpec(memory_space=pltpu.VMEM),
        scratch_shapes=[
            pltpu.VMEM(slots, jnp.bfloat16),
            pltpu.VMEM(slots, jnp.bfloat16),
            pltpu.VMEM(slots, jnp.bfloat16),
            pltpu.VMEM(post_norm.shape, jnp.float32),
        ]
        + [pltpu.SemaphoreType.DMA((groups - 1,))] * 4,
        cost_estimate=pl.CostEstimate(
            flops=6 * groups * post_norm.shape[0] * gate.size,
            bytes_accessed=2**24,
            transcendentals=0,
        ),
        compiler_params=pltpu.CompilerParams(
            collective_id=1, has_side_effects=True, vmem_limit_bytes=48 * 2**20
        ),
    )(post_norm, residual, gate, up, down)


def widened(key_rows, live, hidden_at):
    rows = jnp.where(live[:, None], key_rows, jnp.zeros_like(key_rows))
    bias = jnp.where(live, 0.0, -1e30).astype(jnp.bfloat16)[:, None]
    between = jnp.zeros((rows.shape[0], MARK - rows.shape[1] - 1), jnp.bfloat16)
    return jnp.concatenate([rows, bias, between, hidden_at], axis=1)


def body(
    tokens,
    input_gain,
    query_down,
    query_gain,
    query_up,
    latent_down,
    latent_gain,
    key_up,
    value_up,
    output_weight,
    post_gain,
    gate_weight,
    up_weight,
    down_weight,
    cache_latents,
    prompt_latents,
    cache_len,
    prompt_len,
    prompt_of,
):
    group_index = lax.axis_index("grp")
    shard_index = lax.axis_index("tok")
    tok_dev = tokens.shape[0]
    tok_count = lax.axis_size("tok")
    group_requests = tok_dev * tok_count // SPAN
    local_request = shard_index % group_requests
    owner = group_index * group_requests + local_request
    offset = shard_index // group_requests * tok_dev
    within = offset + jnp.arange(tok_dev, dtype=jnp.int32)
    own_prompt = prompt_of[owner]
    prompt_live = prompt_len[own_prompt]
    cache_live = cache_len[owner]
    positions = prompt_live + cache_live + within
    normed = norm_rows(tokens.astype(jnp.float32), input_gain).astype(jnp.bfloat16)
    query_latent = norm_rows(
        jnp.dot(normed, query_down, preferred_element_type=jnp.float32), query_gain
    ).astype(jnp.bfloat16)
    query_full = jnp.dot(query_latent, query_up, preferred_element_type=jnp.float32).astype(
        jnp.bfloat16
    )
    query_full = lax.optimization_barrier(query_full).reshape(tok_dev, HEADS, NOPE + ROPE)
    score_scale = 1.4426950408889634 / (NOPE + ROPE) ** 0.5
    absorbed = jnp.einsum(
        "thd,khd->htk",
        query_full[..., :NOPE],
        key_up.reshape(KVR, HEADS, NOPE),
        preferred_element_type=jnp.float32,
    )
    turned = rotate(query_full[..., NOPE:].astype(jnp.float32), positions).transpose(1, 0, 2)
    queries = (jnp.concatenate([absorbed, turned], axis=-1) * score_scale).astype(jnp.bfloat16)
    marks = jnp.concatenate(
        [
            jnp.ones((tok_dev, 1), jnp.bfloat16),
            jnp.zeros((tok_dev, MARK - KVR - ROPE - 1), jnp.bfloat16),
            jnp.eye(tok_dev, dtype=jnp.bfloat16),
        ],
        axis=1,
    )
    query_rows = jnp.concatenate(
        [queries, jnp.broadcast_to(marks, (HEADS,) + marks.shape)], axis=-1
    ).reshape(HEADS * tok_dev, MARK + tok_dev)
    latent_raw = jnp.dot(normed, latent_down, preferred_element_type=jnp.float32)
    new_latents = jnp.concatenate(
        [norm_rows(latent_raw[:, :KVR], latent_gain), rotate(latent_raw[:, KVR:], positions)],
        axis=-1,
    ).astype(jnp.bfloat16)
    group_prompts = jnp.concatenate(
        [
            lax.dynamic_slice_in_dim(
                prompt_latents, prompt_of[group_index * group_requests + each], 1, 0
            )
            for each in range(group_requests)
        ],
        axis=0,
    )
    cache_all = lax.all_gather(cache_latents, "tok", axis=1, tiled=True)
    prompt_all = lax.all_gather(group_prompts, "tok", axis=1, tiled=True)
    span_all = lax.all_gather(new_latents, "tok", axis=0)
    cache_rows = lax.dynamic_index_in_dim(cache_all, local_request, 0, keepdims=False)
    prompt_rows = lax.dynamic_index_in_dim(prompt_all, local_request, 0, keepdims=False)
    span_rows = lax.dynamic_index_in_dim(
        span_all.reshape(SPAN // tok_dev, group_requests, tok_dev, KVR + ROPE),
        local_request,
        1,
        keepdims=False,
    ).reshape(SPAN, KVR + ROPE)
    span_place = jnp.arange(SPAN, dtype=jnp.int32)
    hidden = jnp.where(span_place[:, None] <= within[None, :], 0.0, -1e30).astype(jnp.bfloat16)
    prompt_live_rows = jnp.arange(prompt_rows.shape[0], dtype=jnp.int32) < prompt_live
    cache_live_rows = jnp.arange(cache_rows.shape[0], dtype=jnp.int32) < cache_live
    latent_out = flash(
        query_rows,
        widened(
            prompt_rows,
            prompt_live_rows,
            jnp.zeros((prompt_rows.shape[0], tok_dev), jnp.bfloat16),
        ),
        widened(
            cache_rows, cache_live_rows, jnp.zeros((cache_rows.shape[0], tok_dev), jnp.bfloat16)
        ),
        widened(span_rows, span_place >= 0, hidden),
    ).reshape(HEADS, tok_dev, KVR)
    heads_out = (
        jnp.einsum(
            "htk,khv->thv",
            latent_out,
            value_up.reshape(KVR, HEADS, VDIM),
            preferred_element_type=jnp.float32,
        )
        .astype(jnp.bfloat16)
        .reshape(tok_dev, HEADS * VDIM)
    )
    attended = jnp.dot(heads_out, output_weight, preferred_element_type=jnp.float32)
    residual = lax.optimization_barrier(
        (tokens.astype(jnp.float32) + attended).astype(jnp.bfloat16)
    )
    post_norm = norm_rows(residual.astype(jnp.float32), post_gain).astype(jnp.bfloat16)
    layer_out = feed_forward(
        post_norm,
        residual,
        lax.all_gather(gate_weight, "tok", axis=0, tiled=True),
        lax.all_gather(up_weight, "tok", axis=0, tiled=True),
        lax.all_gather(down_weight, "tok", axis=1, tiled=True),
    )
    return (layer_out, new_latents)


def solution(mesh):
    in_specs = (
        P(("grp", "tok"), None),
        P(),
        P(),
        P(),
        P(),
        P(),
        P(),
        P(),
        P(),
        P(),
        P(),
        P("tok", "grp"),
        P("tok", "grp"),
        P("grp", "tok"),
        P("grp", "tok", None),
        P(None, "tok", None),
        P(),
        P(),
        P(),
    )
    out_specs = (P(("grp", "tok"), None), P(("grp", "tok"), None))
    return jax.shard_map(body, mesh=mesh, in_specs=in_specs, out_specs=out_specs, check_vma=False)
```

```python
import functools

import jax
import jax.numpy as jnp
from jax import lax
from jax.experimental import pallas as pl
from jax.experimental.pallas import tpu as pltpu
from jax.sharding import PartitionSpec as P

KVR = 256
HEADS = 20
NOPE = 64
ROPE = 32
VDIM = 64
SPAN = 1024
MARK = 384


EPSILON = 1e-06


def norm_rows(values, gain_vector):
    mean_square = jnp.mean(values * values, axis=-1, keepdims=True)
    return values * lax.rsqrt(mean_square + EPSILON) * gain_vector.astype(jnp.float32)


def rotate(values, positions):
    half_width = values.shape[-1] // 2
    frequency = 10000.0 ** (-jnp.arange(half_width, dtype=jnp.float32) / half_width)
    angles = positions.astype(jnp.float32)[:, None] * frequency[None, :]
    if values.ndim == 3:
        angles = angles[:, None, :]
    cosine = jnp.cos(angles)
    sine_part = jnp.sin(angles)
    leading = values[..., :half_width]
    trailing = values[..., half_width:]
    return jnp.concatenate(
        [leading * cosine - trailing * sine_part, trailing * cosine + leading * sine_part], axis=-1
    )


def flash_kernel(
    row_block, key_block, q_ref, prompt_ref, cache_ref, span_ref, shard_ref,
    out_ref, whole_ref, own_sem, send_sem, recv_sem,
):
    devices = whole_ref.shape[0]
    me = lax.axis_index("tok")

    def shard_copy(step):
        return pltpu.make_async_remote_copy(
            src_ref=shard_ref,
            dst_ref=whole_ref.at[me],
            send_sem=send_sem.at[step - 1],
            recv_sem=recv_sem.at[step - 1],
            device_id={"tok": lax.rem(me + step, devices)},
            device_id_type=pl.DeviceIdType.MESH,
        )

    own_copy = pltpu.make_async_copy(shard_ref, whole_ref.at[me], own_sem)
    own_copy.start()
    barrier = pltpu.get_barrier_semaphore()
    for step in range(1, devices):
        pl.semaphore_signal(
            barrier,
            inc=1,
            device_id={"tok": lax.rem(me + step, devices)},
            device_id_type=pl.DeviceIdType.MESH,
        )
    pl.semaphore_wait(barrier, devices - 1)
    for step in range(1, devices):
        shard_copy(step).start()
    segments = []
    for ref in (prompt_ref, cache_ref, span_ref):
        for first in range(0, ref.shape[0], key_block):
            segments.append(ref.at[pl.ds(first, min(key_block, ref.shape[0]))])

    @pl.loop(0, q_ref.shape[0] // row_block)
    def _(step):
        rows = pl.ds(pl.multiple_of(step * row_block, row_block), row_block)
        q = q_ref[rows, :]

        def score(keys):
            return lax.dot_general(
                q, keys[...], (((1,), (1,)), ((), ())), preferred_element_type=jnp.float32
            )

        scores = score(segments[0])
        largest = None
        for at, keys in enumerate(segments):
            following = score(segments[at + 1]) if at + 1 < len(segments) else None
            block_max = jnp.max(scores, axis=1, keepdims=True)
            new_max = block_max if at == 0 else jnp.maximum(largest, block_max)
            weights = jnp.exp2(scores - new_max)
            block_sum = jnp.sum(weights, axis=1, keepdims=True)
            product = jnp.dot(
                weights.astype(jnp.bfloat16), keys[:, :KVR], preferred_element_type=jnp.float32
            )
            if at == 0:
                total, mixed = block_sum, product
            else:
                factor = jnp.exp2(largest - new_max)
                total = total * factor + block_sum
                mixed = mixed * factor + product
            largest, scores = new_max, following
        out_ref[rows, :] = (mixed / total).astype(jnp.bfloat16)

    own_copy.wait()
    for step in range(1, devices):
        shard_copy(step).wait()


def flash(queries, prompt_keys, cache_keys, span_keys, shard):
    devices = lax.axis_size("tok")
    rows = queries.shape[0]
    count = prompt_keys.shape[0] + cache_keys.shape[0] + span_keys.shape[0]
    return pl.pallas_call(
        functools.partial(flash_kernel, 512, 512),
        out_shape=(
            jax.ShapeDtypeStruct((rows, KVR), jnp.bfloat16),
            jax.ShapeDtypeStruct((devices,) + shard.shape, shard.dtype),
        ),
        in_specs=[pl.BlockSpec(memory_space=pltpu.VMEM)] * 4
        + [pl.BlockSpec(memory_space=pl.ANY)],
        out_specs=(
            pl.BlockSpec(memory_space=pltpu.VMEM),
            pl.BlockSpec(memory_space=pl.ANY),
        ),
        scratch_shapes=[
            pltpu.SemaphoreType.DMA,
            pltpu.SemaphoreType.DMA((devices - 1,)),
            pltpu.SemaphoreType.DMA((devices - 1,)),
        ],
        cost_estimate=pl.CostEstimate(
            flops=2 * rows * count * 768, bytes_accessed=2**24, transcendentals=rows * count
        ),
        compiler_params=pltpu.CompilerParams(
            collective_id=2, has_side_effects=True, vmem_limit_bytes=48 * 2**20
        ),
    )(queries, prompt_keys, cache_keys, span_keys, shard)


def feed_forward_kernel(
    post_ref, residual_ref, gate_ref, up_ref, down_ref, out_ref,
    rows_in, part_out, part_in, own, row_send, row_recv, part_send, part_recv,
):
    groups = rows_in.shape[0] + 1
    me = lax.axis_index("grp")

    def device(step):
        return {"grp": lax.rem(me + step + groups, groups)}

    def row_copy(step):
        return pltpu.make_async_remote_copy(
            src_ref=post_ref,
            dst_ref=rows_in.at[step - 1],
            send_sem=row_send.at[step - 1],
            recv_sem=row_recv.at[step - 1],
            device_id=device(step),
            device_id_type=pl.DeviceIdType.MESH,
        )

    def part_copy(step):
        return pltpu.make_async_remote_copy(
            src_ref=part_out.at[step - 1],
            dst_ref=part_in.at[step - 1],
            send_sem=part_send.at[step - 1],
            recv_sem=part_recv.at[step - 1],
            device_id=device(-step),
            device_id_type=pl.DeviceIdType.MESH,
        )

    def layer(rows):
        gate = jnp.dot(rows, gate_ref[...], preferred_element_type=jnp.float32)
        up = jnp.dot(rows, up_ref[...], preferred_element_type=jnp.float32)
        hidden = (gate / (1.0 + jnp.exp(-gate)) * up).astype(jnp.bfloat16)
        return jnp.dot(hidden, down_ref[...], preferred_element_type=jnp.float32)

    barrier = pltpu.get_barrier_semaphore()
    for step in range(1, groups):
        pl.semaphore_signal(
            barrier, inc=1, device_id=device(step), device_id_type=pl.DeviceIdType.MESH
        )
    pl.semaphore_wait(barrier, groups - 1)
    for step in range(1, groups):
        row_copy(step).start()
    own[...] = layer(post_ref[...]) + residual_ref[...].astype(jnp.float32)

    @pl.loop(1, groups)
    def _(step):
        row_copy(step).wait_recv()
        part_out[step - 1] = layer(rows_in[step - 1]).astype(jnp.bfloat16)
        part_copy(step).start()

    @pl.loop(1, groups)
    def _(step):
        part_copy(step).wait_recv()
        own[...] += part_in[step - 1].astype(jnp.float32)
        part_copy(step).wait_send()
        row_copy(step).wait_send()

    out_ref[...] = own[...].astype(jnp.bfloat16)


def feed_forward(post_norm, residual, gate, up, down):
    groups = lax.axis_size("grp")
    slots = (groups - 1,) + post_norm.shape
    return pl.pallas_call(
        feed_forward_kernel,
        out_shape=jax.ShapeDtypeStruct(post_norm.shape, jnp.bfloat16),
        in_specs=[pl.BlockSpec(memory_space=pltpu.VMEM)] * 5,
        out_specs=pl.BlockSpec(memory_space=pltpu.VMEM),
        scratch_shapes=[
            pltpu.VMEM(slots, jnp.bfloat16),
            pltpu.VMEM(slots, jnp.bfloat16),
            pltpu.VMEM(slots, jnp.bfloat16),
            pltpu.VMEM(post_norm.shape, jnp.float32),
        ]
        + [pltpu.SemaphoreType.DMA((groups - 1,))] * 4,
        cost_estimate=pl.CostEstimate(
            flops=6 * groups * post_norm.shape[0] * gate.size,
            bytes_accessed=2**24,
            transcendentals=0,
        ),
        compiler_params=pltpu.CompilerParams(
            collective_id=1, has_side_effects=True, vmem_limit_bytes=48 * 2**20
        ),
    )(post_norm, residual, gate, up, down)


def widened(key_rows, live, hidden_at):
    rows = jnp.where(live[:, None], key_rows, jnp.zeros_like(key_rows))
    bias = jnp.where(live, 0.0, -1e30).astype(jnp.bfloat16)[:, None]
    between = jnp.zeros((rows.shape[0], MARK - rows.shape[1] - 1), jnp.bfloat16)
    return jnp.concatenate([rows, bias, between, hidden_at], axis=1)


def body(
    tokens,
    input_gain,
    query_down,
    query_gain,
    query_up,
    latent_down,
    latent_gain,
    key_up,
    value_up,
    output_weight,
    post_gain,
    gate_weight,
    up_weight,
    down_weight,
    cache_latents,
    prompt_latents,
    cache_len,
    prompt_len,
    prompt_of,
):
    group_index = lax.axis_index("grp")
    shard_index = lax.axis_index("tok")
    tok_dev = tokens.shape[0]
    tok_count = lax.axis_size("tok")
    group_requests = tok_dev * tok_count // SPAN
    local_request = shard_index % group_requests
    owner = group_index * group_requests + local_request
    offset = shard_index // group_requests * tok_dev
    within = offset + jnp.arange(tok_dev, dtype=jnp.int32)
    own_prompt = prompt_of[owner]
    prompt_live = prompt_len[own_prompt]
    cache_live = cache_len[owner]
    positions = prompt_live + cache_live + within
    normed = norm_rows(tokens.astype(jnp.float32), input_gain).astype(jnp.bfloat16)
    query_latent = norm_rows(
        jnp.dot(normed, query_down, preferred_element_type=jnp.float32), query_gain
    ).astype(jnp.bfloat16)
    query_full = jnp.dot(query_latent, query_up, preferred_element_type=jnp.float32).astype(
        jnp.bfloat16
    )
    query_full = lax.optimization_barrier(query_full).reshape(tok_dev, HEADS, NOPE + ROPE)
    score_scale = 1.4426950408889634 / (NOPE + ROPE) ** 0.5
    absorbed = jnp.einsum(
        "thd,khd->htk",
        query_full[..., :NOPE],
        key_up.reshape(KVR, HEADS, NOPE),
        preferred_element_type=jnp.float32,
    )
    turned = rotate(query_full[..., NOPE:].astype(jnp.float32), positions).transpose(1, 0, 2)
    queries = (jnp.concatenate([absorbed, turned], axis=-1) * score_scale).astype(jnp.bfloat16)
    marks = jnp.concatenate(
        [
            jnp.ones((tok_dev, 1), jnp.bfloat16),
            jnp.zeros((tok_dev, MARK - KVR - ROPE - 1), jnp.bfloat16),
            jnp.eye(tok_dev, dtype=jnp.bfloat16),
        ],
        axis=1,
    )
    query_rows = jnp.concatenate(
        [queries, jnp.broadcast_to(marks, (HEADS,) + marks.shape)], axis=-1
    ).reshape(HEADS * tok_dev, MARK + tok_dev)
    latent_raw = jnp.dot(normed, latent_down, preferred_element_type=jnp.float32)
    new_latents = jnp.concatenate(
        [norm_rows(latent_raw[:, :KVR], latent_gain), rotate(latent_raw[:, KVR:], positions)],
        axis=-1,
    ).astype(jnp.bfloat16)
    group_prompts = jnp.concatenate(
        [
            lax.dynamic_slice_in_dim(
                prompt_latents, prompt_of[group_index * group_requests + each], 1, 0
            )
            for each in range(group_requests)
        ],
        axis=0,
    )
    cache_all = lax.all_gather(cache_latents, "tok", axis=1, tiled=True)
    prompt_all = lax.all_gather(group_prompts, "tok", axis=1, tiled=True)
    span_all = lax.all_gather(new_latents, "tok", axis=0)
    cache_rows = lax.dynamic_index_in_dim(cache_all, local_request, 0, keepdims=False)
    prompt_rows = lax.dynamic_index_in_dim(prompt_all, local_request, 0, keepdims=False)
    span_rows = lax.dynamic_index_in_dim(
        span_all.reshape(SPAN // tok_dev, group_requests, tok_dev, KVR + ROPE),
        local_request,
        1,
        keepdims=False,
    ).reshape(SPAN, KVR + ROPE)
    span_place = jnp.arange(SPAN, dtype=jnp.int32)
    hidden = jnp.where(span_place[:, None] <= within[None, :], 0.0, -1e30).astype(jnp.bfloat16)
    prompt_live_rows = jnp.arange(prompt_rows.shape[0], dtype=jnp.int32) < prompt_live
    cache_live_rows = jnp.arange(cache_rows.shape[0], dtype=jnp.int32) < cache_live
    latent_out, up_all = flash(
        query_rows,
        widened(
            prompt_rows,
            prompt_live_rows,
            jnp.zeros((prompt_rows.shape[0], tok_dev), jnp.bfloat16),
        ),
        widened(
            cache_rows, cache_live_rows, jnp.zeros((cache_rows.shape[0], tok_dev), jnp.bfloat16)
        ),
        widened(span_rows, span_place >= 0, hidden),
        up_weight,
    )
    latent_out = latent_out.reshape(HEADS, tok_dev, KVR)
    heads_out = (
        jnp.einsum(
            "htk,khv->thv",
            latent_out,
            value_up.reshape(KVR, HEADS, VDIM),
            preferred_element_type=jnp.float32,
        )
        .astype(jnp.bfloat16)
        .reshape(tok_dev, HEADS * VDIM)
    )
    attended = jnp.dot(heads_out, output_weight, preferred_element_type=jnp.float32)
    residual = lax.optimization_barrier(
        (tokens.astype(jnp.float32) + attended).astype(jnp.bfloat16)
    )
    post_norm = norm_rows(residual.astype(jnp.float32), post_gain).astype(jnp.bfloat16)
    layer_out = feed_forward(
        post_norm,
        residual,
        lax.all_gather(gate_weight, "tok", axis=0, tiled=True),
        up_all.reshape(-1, up_weight.shape[1]),
        lax.all_gather(down_weight, "tok", axis=1, tiled=True),
    )
    return (layer_out, new_latents)


def solution(mesh):
    in_specs = (
        P(("grp", "tok"), None),
        P(),
        P(),
        P(),
        P(),
        P(),
        P(),
        P(),
        P(),
        P(),
        P(),
        P("tok", "grp"),
        P("tok", "grp"),
        P("grp", "tok"),
        P("grp", "tok", None),
        P(None, "tok", None),
        P(),
        P(),
        P(),
    )
    out_specs = (P(("grp", "tok"), None), P(("grp", "tok"), None))
    return jax.shard_map(body, mesh=mesh, in_specs=in_specs, out_specs=out_specs, check_vma=False)
```
